32 devices in a mesh: circ: 4 (over z), axial: 8 (over y, x, core).
Axes of the slice: x: 2, y: 2, z: 4, core: 2. Of those that a mesh axis runs over, the one named last changes fastest.
Arguments:
- position: float32 [3, 4, 8, 16384], P(None, 'circ', 'axial'), may hold values from -3 to 3
- displacement: float32 [3, 4, 8, 16384], P(None, 'circ', 'axial'), may hold values from -3 to 3
- velocity: float32 [3, 4, 8, 16384], P(None, 'circ', 'axial'), may hold values from -1.5 to 1.5
- bulk: float32 [4, 8, 16384], P('circ', 'axial'), may hold values from 6 to 30
- shear: float32 [4, 8, 16384], P('circ', 'axial'), may hold values from 0.5 to 2
- volume: float32 [4, 8, 16384], P('circ', 'axial'), may hold values from 60 to 200
- edges: int32 [4, 8, 2, 32], P('circ', 'axial'), may hold values from 0 to 127, as said below
- block_pairs: int32 [4, 8, 2, 320], P('circ', 'axial'), may hold values from 0 to 191, as said below
- block_counts: int32 [4, 8, 2], P('circ', 'axial'), may hold values from 128 to 320, as said below
- damage: int32 [4, 8, 320, 128, 128], P('circ', 'axial'), may hold values 0 or 1
Outputs:
- final_displacement: float32 [3, 4, 8, 16384], P(None, 'circ', 'axial')
- final_velocity: float32 [3, 4, 8, 16384], P(None, 'circ', 'axial')
- dilatation: float32 [4, 8, 16384], P('circ', 'axial')
The draws below stay inside these ranges and needn't reach their ends.
Inputs may be any that keep to these rules, and one draw needn't show every extreme that they name: `edges`: for each device the 64 entries are distinct clusters of that device. `block_pairs`: slot b below 128 pairs cluster b with itself; the further slots below block_counts[c, a, 0] pair two different clusters of the device; the next slots up to block_counts[c, a, 1] are cross blocks whose target is an extended slot of 128 or more, each extended slot of the device's neighbours used exactly once (only the circumferential ones on the last axial section); later slots hold unused pairs of two different local clusters. `block_counts`: entry 0 is the number of local blocks, 128 or more; entry 1 the number of all blocks of the device, which is 32 or 64 more than entry 0.
All inputs are finite; a program needn't handle non-finite values. No bound on the sum of `damage` on one device may be relied on, other than what follows from the above.
Results may differ from the reference program's by a relative error of at most 0.0003.
Values sent between devices are 32-bit elements; how exact they have to be, the bound alone decides.
A program may use at most 64 MiB of HBM per device.

```python
import math
import jax
import jax.numpy as jnp
from jax import lax

CLUSTER_PTS = 128
CLUSTERS = 128
FACING = 32
GROUP_SLOTS = 16
TIME_STEPS = 2
BLOCK_SLOTS = 320
SECTORS = 4
SECTIONS = 8
POINTS_DEV = 16384


def draw_edges(key, part):
    device_keys = jax.random.split(jax.random.fold_in(key, 3), SECTORS * SECTIONS)

    def one_device(device_key):
        order = jax.random.permutation(device_key, CLUSTERS).astype(jnp.int32)
        return order[:2 * FACING].reshape(2, FACING)
    return jax.vmap(one_device)(device_keys).reshape(SECTORS, SECTIONS, 2, FACING)


def block_layout(key):
    base_key = jax.random.fold_in(key, 7)
    crack_key, count_key, pair_key = jax.random.split(base_key, 3)
    crack_circ = jax.random.randint(crack_key, (), 0, SECTORS)
    crack_axial = jax.random.randint(jax.random.fold_in(crack_key, 1), (), 0, SECTIONS)
    circ_index = jnp.arange(SECTORS, dtype=jnp.int32)[:, None]
    axial_index = jnp.arange(SECTIONS, dtype=jnp.int32)[None, :]
    in_crack = ((circ_index - crack_circ) % SECTORS <= 1) & (jnp.abs(axial_index - crack_axial) <= SECTIONS // 4)
    last_section = (axial_index == SECTIONS - 1) & (circ_index >= 0)
    cross_count = jnp.where(last_section, FACING, 2 * FACING)
    quiet = CLUSTERS + jax.random.randint(count_key, (SECTORS, SECTIONS), CLUSTERS // 4, CLUSTERS // 2 + 1)
    local_count = jnp.where(in_crack, BLOCK_SLOTS - cross_count, quiet).astype(jnp.int32)
    total_count = (local_count + cross_count).astype(jnp.int32)
    device_keys = jax.random.split(pair_key, SECTORS * SECTIONS)

    def one_device(device_key, local_number, is_last):
        order_key, offset_key, source_key, both_key, circ_key = jax.random.split(device_key, 5)
        slot_index = jnp.arange(BLOCK_SLOTS, dtype=jnp.int32)
        order = jax.random.permutation(order_key, CLUSTERS).astype(jnp.int32)
        offsets = jax.random.randint(offset_key, (BLOCK_SLOTS,), 1, 4).astype(jnp.int32)
        extra_index = jnp.maximum(slot_index - CLUSTERS, 0) % CLUSTERS
        extra_source = order[extra_index]
        is_self = slot_index < CLUSTERS
        local_source = jnp.where(is_self, slot_index, extra_source)
        local_target = jnp.where(is_self, slot_index, (extra_source + offsets) % CLUSTERS)
        cross_sources = jax.random.permutation(source_key, CLUSTERS).astype(jnp.int32)
        both_order = jax.random.permutation(both_key, 2 * FACING).astype(jnp.int32)
        circ_order = jax.random.permutation(circ_key, FACING).astype(jnp.int32)
        cross_slot = slot_index - local_number
        crossing = (cross_slot >= 0) & (cross_slot < jnp.where(is_last, FACING, 2 * FACING))
        picked = jnp.where(is_last, circ_order[jnp.clip(cross_slot, 0, FACING - 1)], both_order[jnp.clip(cross_slot, 0, 2 * FACING - 1)])
        source_ids = jnp.where(crossing, cross_sources[jnp.clip(cross_slot, 0, CLUSTERS - 1)], local_source)
        target_ids = jnp.where(crossing, CLUSTERS + picked, local_target)
        return jnp.stack([source_ids, target_ids]).astype(jnp.int32)
    pairs = jax.vmap(one_device)(device_keys, local_count.reshape(-1), last_section.reshape(-1))
    return (local_count, total_count, pairs.reshape(SECTORS, SECTIONS, 2, BLOCK_SLOTS))


def draw_block_pairs(key, part):
    return block_layout(key)[2]


def draw_block_counts(key, part):
    local_count, total_count, pairs = block_layout(key)
    return jnp.stack([local_count, total_count], axis=-1).astype(jnp.int32)


def plant(array, stream_key, smallest, high):
    index_at = [jax.random.randint(jax.random.fold_in(stream_key, axis), (), 0, length) for axis, length in enumerate(array.shape)]
    widest = array.shape.index(max(array.shape))
    beside = index_at[:widest] + [(index_at[widest] + 1) % array.shape[widest]] + index_at[widest + 1:]
    return array.at[tuple(index_at)].set(smallest).at[tuple(beside)].set(high)


def shard_levels(rng, shape, shards, least, top_value):
    factor_of = 1.0
    for axis_at, blocks in shards:
        draws = jax.random.uniform(jax.random.fold_in(jax.random.fold_in(rng, 6), axis_at), (blocks,), jnp.float32, least / len(shards), top_value / len(shards))
        factor_of = factor_of * jnp.repeat(jnp.exp(draws), shape[axis_at] // blocks).reshape((-1,) + (1,) * (len(shape) - 1 - axis_at))
    return factor_of


def centred(stream_key, dims, deviation, most, pieces=(), kind=jnp.bfloat16):
    gain = shard_levels(stream_key, dims, pieces, -0.22, 0.18) if pieces else 1.0
    drawn = jax.random.normal(stream_key, dims, jnp.float32) * deviation * gain
    return jnp.minimum(jnp.maximum(drawn, -most), most).astype(kind)


def setup_inputs(seed: int = 0) -> dict:
    arg_keys = jax.random.split(jax.random.key(seed), 11)
    return {
        "position": centred(arg_keys[0], (3, SECTORS, SECTIONS, POINTS_DEV), 0.5, 3.0, ((1, 4), (2, 8)), jnp.float32),
        "displacement": centred(arg_keys[1], (3, SECTORS, SECTIONS, POINTS_DEV), 0.5, 3.0, ((1, 4), (2, 8)), jnp.float32),
        "velocity": centred(arg_keys[2], (3, SECTORS, SECTIONS, POINTS_DEV), 0.2, 1.5, ((1, 4), (2, 8)), jnp.float32),
        "bulk": jnp.clip(jnp.exp(math.log(30.0) - 1.609438 * jax.random.uniform(arg_keys[3], (SECTORS, SECTIONS, POINTS_DEV), jnp.float32) ** shard_levels(arg_keys[3], (SECTORS, SECTIONS, POINTS_DEV), ((0, 4), (1, 8)), -0.2, 0.2)), 6.0, 30.0),
        "shear": jnp.clip(jnp.exp(math.log(2.0) - 1.3862944 * jax.random.uniform(arg_keys[4], (SECTORS, SECTIONS, POINTS_DEV), jnp.float32) ** shard_levels(arg_keys[4], (SECTORS, SECTIONS, POINTS_DEV), ((0, 4), (1, 8)), -0.2, 0.2)), 0.5, 2.0),
        "volume": jnp.clip(jnp.exp(math.log(200.0) - 1.2039728 * jax.random.uniform(arg_keys[5], (SECTORS, SECTIONS, POINTS_DEV), jnp.float32) ** shard_levels(arg_keys[5], (SECTORS, SECTIONS, POINTS_DEV), ((0, 4), (1, 8)), -0.2, 0.2)), 60.0, 200.0),
        "edges": draw_edges(jax.random.fold_in(arg_keys[10], 71), 0),
        "block_pairs": draw_block_pairs(jax.random.fold_in(arg_keys[10], 71), 0),
        "block_counts": draw_block_counts(jax.random.fold_in(arg_keys[10], 71), 0),
        "damage": plant((jax.random.randint(arg_keys[9], (SECTORS, SECTIONS, BLOCK_SLOTS, CLUSTER_PTS, CLUSTER_PTS), 0, 20) < 17).astype(jnp.int32), jax.random.fold_in(arg_keys[9], 1), 0, 1),
    }


SOFTEN = 0.01
HORIZON_SQ = 1.0
TIMESTEP = 0.07

def bond_geometry(source, target):
    spacing = target[:, 0:3, None, :] - source[:, 0:3, :, None]
    relative = target[:, 3:6, None, :] - source[:, 3:6, :, None]
    stretched = spacing + relative
    length_sq = lax.optimization_barrier(jnp.sum(spacing * spacing, axis=1))
    deformed_sq = lax.optimization_barrier(jnp.sum(stretched * stretched, axis=1))
    length = jnp.sqrt(length_sq)
    extension = jnp.sqrt(deformed_sq) - length
    influence = jnp.exp(-length_sq / HORIZON_SQ)
    return (stretched, deformed_sq, length, extension, influence)

def bond_pass(source, target, weight, phase_no):
    stretched, deformed_sq, length, extension, influence = bond_geometry(source, target)
    if phase_no == 1:
        bond_term = weight * influence * length * extension
        return (lax.optimization_barrier(jnp.sum(bond_term, axis=2))[:, None, :], lax.optimization_barrier(jnp.sum(bond_term, axis=1))[:, None, :])
    own_state = influence * (source[:, 6, :, None] * source[:, 8, :, None] * length + source[:, 7, :, None] * extension)
    other_state = influence * (target[:, 6, None, :] * target[:, 8, None, :] * length + target[:, 7, None, :] * extension)
    magnitude = weight * (own_state + other_state) / jnp.sqrt(deformed_sq + SOFTEN)
    bond_force = magnitude[:, None] * stretched
    return (lax.optimization_barrier(jnp.sum(bond_force, axis=3)), -lax.optimization_barrier(jnp.sum(bond_force, axis=2)))

def bond_weight(source_ids, target_ids, usable, damage_slab):
    points = damage_slab.shape[-1]
    upper_tri = lax.broadcasted_iota(jnp.int32, (points, points), 0) < lax.broadcasted_iota(jnp.int32, (points, points), 1)
    keeper = jnp.where((source_ids == target_ids)[:, None, None], upper_tri[None], True)
    keeper = keeper & usable[:, None, None]
    return jnp.where(keeper, damage_slab.astype(jnp.float32), jnp.zeros(damage_slab.shape, jnp.float32))

def device_pass(inputs, phase_no, row_width):
    point_table, source_list, target_list, total_count, damage_all = inputs
    extent = point_table.shape[0]

    def turn(group_index, accumulated):
        first_slot = group_index * GROUP_SLOTS
        slot_ids = first_slot + jnp.arange(GROUP_SLOTS, dtype=jnp.int32)
        usable = slot_ids < total_count
        source_ids = jnp.where(usable, lax.dynamic_slice_in_dim(source_list, first_slot, GROUP_SLOTS), 0)
        target_ids = jnp.where(usable, lax.dynamic_slice_in_dim(target_list, first_slot, GROUP_SLOTS), 0)
        damage_slab = lax.dynamic_slice_in_dim(damage_all, first_slot, GROUP_SLOTS)
        weight = bond_weight(source_ids, target_ids, usable, damage_slab)
        source_part, target_part = bond_pass(point_table[source_ids], point_table[target_ids], weight, phase_no)
        return accumulated.at[source_ids].add(source_part).at[target_ids].add(target_part)
    empty = jnp.zeros((extent, row_width, point_table.shape[-1]), jnp.float32)
    return lax.fori_loop(0, (total_count + GROUP_SLOTS - 1) // GROUP_SLOTS, turn, empty)

def all_devices(full_table, source_lists, target_lists, totals, slabs, phase_no, row_width):
    devices = SECTORS * SECTIONS
    flat_table = full_table.reshape((devices,) + full_table.shape[2:])
    result = lax.map(lambda inputs: device_pass(inputs, phase_no, row_width), (flat_table, source_lists, target_lists, totals, slabs))
    return result.reshape((SECTORS, SECTIONS) + result.shape[1:])

def clustered(quantity):
    row_count = quantity.shape[0]
    shaped = quantity.reshape(row_count, SECTORS, SECTIONS, CLUSTERS, CLUSTER_PTS)
    return jnp.transpose(shaped, (1, 2, 3, 0, 4))

def flattened(quantity):
    row_count = quantity.shape[3]
    return jnp.transpose(quantity, (3, 0, 1, 2, 4)).reshape(row_count, SECTORS, SECTIONS, POINTS_DEV)

def facing(stacked, edges):
    upper_rows = jnp.roll(stacked, -1, axis=0)
    upper_ids = jnp.roll(edges[:, :, 0], -1, axis=0)
    after_rows = jnp.concatenate([stacked[:, 1:], jnp.zeros_like(stacked[:, :1])], axis=1)
    after_ids = jnp.concatenate([edges[:, 1:, 1], jnp.zeros_like(edges[:, :1, 1])], axis=1)
    shape_out = upper_ids.shape + stacked.shape[3:]
    upward = jnp.take_along_axis(upper_rows, jnp.broadcast_to(upper_ids[:, :, :, None, None], shape_out), axis=2)
    axially = jnp.take_along_axis(after_rows, jnp.broadcast_to(after_ids[:, :, :, None, None], shape_out), axis=2)
    return (upward, axially)

def returned(partials, edges):
    local_part = partials[:, :, :CLUSTERS]
    upward = jnp.roll(partials[:, :, CLUSTERS:CLUSTERS + FACING], 1, axis=0)
    before = partials[:, :, CLUSTERS + FACING:]
    axially = jnp.concatenate([jnp.zeros_like(before[:, :1]), before[:, :-1]], axis=1)
    cluster_ids = jnp.arange(CLUSTERS, dtype=jnp.int32)
    circ_hot = (edges[:, :, 0, :, None] == cluster_ids).astype(jnp.float32)
    axial_hot = (edges[:, :, 1, :, None] == cluster_ids).astype(jnp.float32)
    from_upper = jnp.einsum('safk,safrc->sakrc', circ_hot, upward, precision=lax.Precision.HIGHEST)
    from_after = jnp.einsum('safk,safrc->sakrc', axial_hot, axially, precision=lax.Precision.HIGHEST)
    return local_part + from_upper + from_after

def reference(position, displacement, velocity, bulk, shear, volume, edges, block_pairs, block_counts, damage):
    point_positions = clustered(position)
    moving_state = clustered(displacement)
    velocities = clustered(velocity)
    bulk_modulus = clustered(bulk[None])
    shear_modulus = clustered(shear[None])
    weighted_volume = clustered(volume[None])
    dilatation_factor = (3.0 * bulk_modulus - 5.0 * shear_modulus) / weighted_volume
    deviatoric_factor = 15.0 * shear_modulus / weighted_volume
    devices = SECTORS * SECTIONS
    pair_lists = block_pairs.reshape(devices, 2, BLOCK_SLOTS)
    totals = block_counts[:, :, 1].reshape(devices)
    slabs = damage.reshape(devices, BLOCK_SLOTS, CLUSTER_PTS, CLUSTER_PTS)
    dilatation = jnp.zeros_like(weighted_volume)
    for step_index in range(TIME_STEPS):
        first_table = jnp.concatenate([point_positions, moving_state], axis=3)
        upward, axially = facing(first_table, edges)
        full_table = jnp.concatenate([first_table, upward, axially], axis=2)
        partials = all_devices(full_table, pair_lists[:, 0], pair_lists[:, 1], totals, slabs, 1, 1)
        dilatation = 3.0 * returned(partials, edges) / weighted_volume
        second_point_table = jnp.concatenate([point_positions, moving_state, dilatation_factor, deviatoric_factor, dilatation], axis=3)
        upward, axially = facing(second_point_table, edges)
        full_table = jnp.concatenate([second_point_table, upward, axially], axis=2)
        partials = all_devices(full_table, pair_lists[:, 0], pair_lists[:, 1], totals, slabs, 2, 3)
        force = returned(partials, edges)
        velocities = velocities + TIMESTEP * force
        moving_state = moving_state + TIMESTEP * velocities
    return (flattened(moving_state), flattened(velocities), flattened(dilatation)[0])
```

```python
import functools
import math

import jax
import jax.numpy as jnp
from jax import lax
from jax.experimental import pallas as pl
from jax.experimental.pallas import tpu as pltpu
from jax.sharding import PartitionSpec as P

TIME_STEPS = 2
SOFTEN = 0.01
TIMESTEP = 0.07
LOG2E = math.log2(math.e)
SCALE = math.sqrt(LOG2E)
TINY = 1e-12
GROUP = 16
UNROLL = 4


def from_behind(block, axis, distance):
    size = lax.axis_size(axis)
    return lax.ppermute(block, axis, [((i - distance) % size, i) for i in range(size)])


def shifted(shard, axis, by):
    size = lax.axis_size(axis)
    pairs = [(i, i + by) for i in range(size) if 0 <= i + by < size]
    return lax.ppermute(shard, axis, pairs)


def split3(x):
    high = x.astype(jnp.bfloat16).astype(jnp.float32)
    mid = (x - high).astype(jnp.bfloat16).astype(jnp.float32)
    return [high, mid, x - high - mid]


def distance_features(vector):
    parts = [split3(x) for x in vector]
    high, mid, low = ([p[k] for p in parts] for k in range(3))
    norm = split3(vector[0] * vector[0] + vector[1] * vector[1] + vector[2] * vector[2])
    ones = [jnp.ones_like(vector[0])] * 3
    left = [-2.0 * x for x in high * 3] + norm + [-2.0 * x for x in mid * 2 + low] + ones
    right = high + mid + low + ones + high + mid + high + norm
    return left, right


def sum_features(value):
    parts = split3(value)
    ones = [jnp.ones_like(value)] * 3
    pad = [jnp.zeros_like(value)] * 2
    return parts + ones + pad, ones + parts + pad


def halves(x):
    high = x.astype(jnp.bfloat16)
    low = (x - high.astype(jnp.float32)).astype(jnp.bfloat16)
    return high, low


def pair_product(left, right_a, right_b):
    upper = jnp.concatenate([right_a, jnp.zeros_like(right_a)], axis=1)
    lower = jnp.concatenate([jnp.zeros_like(right_b), right_b], axis=1)
    both = jnp.concatenate([upper, lower], axis=0).astype(jnp.bfloat16)
    return lax.dot_general(
        left.astype(jnp.bfloat16),
        both,
        (((0,), (0,)), ((), ())),
        preferred_element_type=jnp.float32,
    )


def pass_kernel(force, first, pairs_ref, count_ref, weight_ref, place_ref, current_ref, *rest):
    rest = list(rest)
    coef_ref = rest.pop(0) if force else None
    out_ref = rest.pop(0)
    kept_ref = rest.pop(0) if first else None
    left_ref, right_ref, acc_ref = rest
    step = pl.program_id(0)
    total = count_ref[1]
    pts = weight_ref.shape[-1]
    extent = place_ref.shape[1]
    width = left_ref.shape[0] // extent
    depth = 16 if force else 8
    rows = 32

    @pl.when(step == 0)
    def _():
        acc_ref[...] = jnp.zeros(acc_ref.shape, jnp.float32)

        def fill(chunk, carry):
            at = pl.ds(pl.multiple_of(chunk * 8, 8), 8)
            groups = [distance_features([place_ref[k, at, :] for k in range(3)])]
            if force:
                groups.append(sum_features(coef_ref[0, at, :]))
            groups.append(distance_features([current_ref[k, at, :] for k in range(3)]))
            if force:
                groups.append(sum_features(coef_ref[1, at, :]))
            left = [x for group in groups for x in group[0]]
            right = [x for group in groups for x in group[1]]
            for k in range(width):
                spot = pl.ds(chunk * (8 * width) + k, 8, stride=width)
                left_ref[spot, :] = left[k]
                right_ref[spot, :] = right[k]
            return carry

        lax.fori_loop(0, extent // 8, fill, 0)

    def one_slot(at):
        slot = step * GROUP + at
        source = pairs_ref[0, slot]
        target = pairs_ref[1, slot]
        used = slot < total
        left = left_ref[pl.ds(pl.multiple_of(source * width, 8), width), :]
        right = right_ref[pl.ds(pl.multiple_of(target * width, 8), width), :]
        if force:
            still = pair_product(left[0:32], right[0:24], right[24:32])
            moved = pair_product(left[32:64], right[32:56], right[56:64])
        else:
            still = pair_product(left, right[0:24], right[24:48])
        highs, lows = [], []
        column_sum = None
        for begin in range(0, pts, rows):
            cut = slice(begin, begin + rows)
            length_sq = jnp.maximum(still[cut, 0:pts], TINY)
            deformed_sq = jnp.maximum(moved[cut, 0:pts] if force else still[cut, pts:], TINY)
            length = length_sq * lax.rsqrt(length_sq)
            extension = deformed_sq * lax.rsqrt(deformed_sq) - length
            weight = weight_ref[at, cut, :]
            if first:
                p = lax.broadcasted_iota(jnp.int32, (rows, pts), 0) + begin
                q = lax.broadcasted_iota(jnp.int32, (rows, pts), 1)
                margin = jnp.where(source == target, 0, -2 * pts)
                weight = jnp.where(p + margin < q, weight.astype(jnp.float32), 0.0)
                weight = weight * jnp.exp2(-length_sq)
                kept_ref[at, cut, :] = weight
            if force:
                state = still[cut, pts:] * length + moved[cut, pts:] * extension
                term = weight * state * lax.rsqrt(deformed_sq + SOFTEN * LOG2E)
            else:
                term = weight * length * extension
                part = jnp.sum(term.reshape(rows // 8, 8, pts), axis=0)
                column_sum = part if column_sum is None else column_sum + part
            high, low = halves(term)
            highs.append(high)
            lows.append(low)
        high = jnp.concatenate(highs, axis=0)
        low = jnp.concatenate(lows, axis=0)
        wide = jnp.concatenate([high, low], axis=1)
        across = (((1,), (1,)), ((), ()))
        if force:
            tall = jnp.concatenate([high, low], axis=0)
            target_rows = right[32:48].astype(jnp.bfloat16)
            begin = pl.multiple_of(source * width, 8) + 32
            source_rows = right_ref[pl.ds(begin, 16), :].astype(jnp.bfloat16)
            to_source = lax.dot_general(
                jnp.concatenate([target_rows, target_rows], axis=1),
                wide,
                across,
                preferred_element_type=jnp.float32,
            )
            to_target = jnp.dot(
                jnp.concatenate([source_rows, source_rows], axis=1),
                tall,
                preferred_element_type=jnp.float32,
            )
        else:
            pick = (lax.broadcasted_iota(jnp.int32, (16, 2 * pts), 0) == 0).astype(jnp.bfloat16)
            to_source = lax.dot_general(pick, wide, across, preferred_element_type=jnp.float32)[0:8]
            to_target = column_sum
        return (
            jnp.where(used, source, extent) * depth,
            jnp.where(used, target, extent) * depth,
            to_source,
            to_target,
        )

    @pl.when(step * GROUP < total)
    def _():
        def turn(index, carry):
            found = [one_slot(index * UNROLL + k) for k in range(UNROLL)]
            for source, target, to_source, to_target in found:
                acc_ref[pl.ds(pl.multiple_of(source, 8), depth), :] += to_source
                acc_ref[pl.ds(pl.multiple_of(target, 8), depth), :] += to_target
            return carry

        lax.fori_loop(0, GROUP // UNROLL, turn, 0)

    @pl.when(step == pl.num_programs(0) - 1)
    def _():
        def finish(chunk, carry):
            at = pl.ds(pl.multiple_of(chunk * 8, 8), 8)

            def row(k):
                return acc_ref[pl.ds(chunk * (8 * depth) + k, 8, stride=depth), :]

            if force:
                count = row(9)
                for k in range(3):
                    moment = row(k) + row(3 + k) + row(6 + k)
                    out_ref[k, at, :] = (moment - current_ref[k, at, :] * count) * (1.0 / SCALE)
            else:
                out_ref[0, at, :] = sum(row(k) for k in range(1, 8)) + row(0)
            return carry

        lax.fori_loop(0, extent // 8, finish, 0)


def run_pass(force, first, pairs, counts, weight, *point_data):
    slots, pts = weight.shape[0], weight.shape[-1]
    extent = point_data[0].shape[1]
    out_rows = 3 if force else 1
    width, depth = (64, 16) if force else (48, 8)

    def slab(i, pairs_ref, count_ref):
        last = (count_ref[1] + GROUP - 1) // GROUP - 1
        return (jnp.minimum(i, last), 0, 0)

    def whole(*_):
        return (0, 0, 0)

    in_specs = [pl.BlockSpec((GROUP, pts, pts), slab)]
    in_specs += [pl.BlockSpec(x.shape, whole, pipeline_mode=pl.Buffered(1)) for x in point_data]
    out_shape = [jax.ShapeDtypeStruct((out_rows, extent, pts), jnp.float32)]
    out_specs = [pl.BlockSpec((out_rows, extent, pts), whole)]
    if first:
        out_shape.append(jax.ShapeDtypeStruct(weight.shape, jnp.float32))
        out_specs.append(pl.BlockSpec((GROUP, pts, pts), slab))
    return pl.pallas_call(
        functools.partial(pass_kernel, force, first),
        grid_spec=pltpu.PrefetchScalarGridSpec(
            num_scalar_prefetch=2,
            grid=(slots // GROUP,),
            in_specs=in_specs,
            out_specs=out_specs,
            scratch_shapes=[
                pltpu.VMEM((extent * width, pts), jnp.float32),
                pltpu.VMEM((extent * width, pts), jnp.float32),
                pltpu.VMEM(((extent + 1) * depth, pts), jnp.float32),
            ],
        ),
        out_shape=out_shape,
        compiler_params=pltpu.CompilerParams(
            dimension_semantics=("arbitrary",), vmem_limit_bytes=48 * 1024 * 1024
        ),
        name="force_pass" if force else "dilatation_pass",
    )(pairs, counts, weight, *point_data)


def body(
    position, displacement, velocity, bulk, shear, volume, edges, block_pairs, block_counts, damage
):
    points = damage.shape[-1]
    clusters = position.shape[-1] // points
    facing = edges.shape[-1]

    def rows_of(quantity):
        return quantity.reshape(-1, clusters, points)

    vol, bulk_c, shear_c = rows_of(volume), rows_of(bulk), rows_of(shear)
    table = jnp.concatenate(
        [
            rows_of(position),
            rows_of(displacement),
            rows_of(velocity),
            (3.0 * bulk_c - 5.0 * shear_c) / vol,
            15.0 * shear_c / vol,
            vol,
        ],
        axis=0,
    )
    pairs = block_pairs[0, 0]
    counts = block_counts[0, 0]
    weight = damage[0, 0]
    hot = (edges[0, 0].reshape(-1)[:, None] == jnp.arange(clusters, dtype=jnp.int32)).astype(
        jnp.float32
    )

    def select(matrix, values):
        return jnp.stack(
            [jnp.dot(matrix, value, precision=lax.Precision.HIGHEST) for value in values]
        )

    def pull(local):
        rows = select(hot, local)
        return jnp.concatenate(
            [from_behind(rows[:, :facing], "circ", -1), shifted(rows[:, facing:], "axial", -1)],
            axis=1,
        )

    def push(halo):
        rows = jnp.concatenate(
            [from_behind(halo[:, :facing], "circ", 1), shifted(halo[:, facing:], "axial", 1)],
            axis=1,
        )
        return select(hot.T, rows)

    def exchanged(partials, last):
        own, halo = partials[:, :clusters], partials[:, clusters:]
        own_sum = own + push(halo)
        halo_sum = halo if last else halo + pull(own)
        return jnp.concatenate([own_sum, halo_sum], axis=1)

    full = jnp.concatenate([table, pull(table)], axis=1)
    place, moving, speed = full[0:3], full[3:6], full[6:9]
    dil_coef, dev_coef, vol = full[9:10], full[10:11], full[11:12]
    vol = jnp.where(vol == 0.0, 1.0, vol)
    still = place * SCALE
    for step in range(TIME_STEPS):
        current = (place + moving) * SCALE
        results = run_pass(False, step == 0, pairs, counts, weight, still, current)
        if step == 0:
            weight = results[1]
        theta = (3.0 / LOG2E) * exchanged(results[0], False) / vol
        coef = jnp.concatenate([dil_coef * theta, dev_coef], axis=0)
        (partials,) = run_pass(True, False, pairs, counts, weight, still, current, coef)
        force = exchanged(partials, step == TIME_STEPS - 1)
        speed = speed + TIMESTEP * force
        moving = moving + TIMESTEP * speed
    return (
        moving[:, :clusters].reshape(displacement.shape),
        speed[:, :clusters].reshape(velocity.shape),
        theta[:, :clusters].reshape(volume.shape),
    )


def solution(mesh):
    wide = P(None, "circ", "axial", None)
    flat = P("circ", "axial", None)
    pairs = P("circ", "axial", None, None)
    return jax.shard_map(
        body,
        mesh=mesh,
        in_specs=(wide, wide, wide, flat, flat, flat, pairs, pairs, flat, P("circ", "axial", None, None, None)),
        out_specs=(wide, wide, flat),
        check_vma=False,
    )
```

```python
import functools
import math

import jax
import jax.numpy as jnp
from jax import lax
from jax.experimental import pallas as pl
from jax.experimental.pallas import tpu as pltpu
from jax.sharding import PartitionSpec as P

TIME_STEPS = 2
SOFTEN = 0.01
TIMESTEP = 0.07
LOG2E = math.log2(math.e)
SCALE = math.sqrt(LOG2E)
TINY = 1e-12
GROUP = 16
UNROLL = 8


def exact_rows(matrix, values):
    parts = jnp.concatenate([x.astype(jnp.bfloat16) for x in split3(values)], axis=0)
    return jnp.dot(matrix, parts, preferred_element_type=jnp.float32)


def exchange_kernel(part_ref, hot_ref, hot_t_ref, out_ref, send_buf, recv_buf, send_sem, recv_sem):
    circ, axial = lax.axis_index("circ"), lax.axis_index("axial")
    circs, axials = lax.axis_size("circ"), lax.axis_size("axial")
    targets = [
        {"circ": lax.rem(circ + circs - 1, circs)},
        {"axial": lax.rem(axial + axials - 1, axials)},
        {"circ": lax.rem(circ + 1, circs)},
        {"axial": lax.rem(axial + 1, axials)},
    ]
    barrier = pltpu.get_barrier_semaphore()
    for device in targets:
        pl.semaphore_signal(
            barrier, inc=1, device_id=device, device_id_type=pl.DeviceIdType.MESH
        )
    row_count, _, pts = part_ref.shape
    clusters = hot_t_ref.shape[0]
    facing = hot_ref.shape[0] // 2

    def copy(k):
        return pltpu.make_async_remote_copy(
            src_ref=send_buf.at[k],
            dst_ref=recv_buf.at[k],
            send_sem=send_sem.at[k],
            recv_sem=recv_sem.at[k],
            device_id=targets[k],
            device_id_type=pl.DeviceIdType.MESH,
        )

    copies = [copy(k) for k in range(4)]
    send_buf[2] = part_ref[:, clusters : clusters + facing, :]
    send_buf[3] = part_ref[:, clusters + facing :, :]
    for r in range(row_count):
        rows = exact_rows(hot_ref[...], part_ref[r, 0:clusters, :])
        send_buf[0, r] = rows[:facing]
        send_buf[1, r] = rows[facing:]
    pl.semaphore_wait(barrier, 4)
    for k in (0, 2, 1, 3):
        copies[k].start()
    for k in (0, 2, 1, 3):
        copies[k].wait()
    has_after = axial < axials - 1
    has_before = axial > 0
    for r in range(row_count):
        halo = part_ref[r, clusters:, :]
        out_ref[r, clusters : clusters + facing, :] = halo[:facing] + recv_buf[0, r]
        out_ref[r, clusters + facing :, :] = halo[facing:] + jnp.where(
            has_after, recv_buf[1, r], 0.0
        )
        arrived = jnp.concatenate(
            [recv_buf[2, r], jnp.where(has_before, recv_buf[3, r], 0.0)], axis=0
        )
        out_ref[r, 0:clusters, :] = part_ref[r, 0:clusters, :] + exact_rows(
            hot_t_ref[...], arrived
        )


def exchange(part, hot, hot_t, collective_id):
    row_count, _, pts = part.shape
    facing = hot.shape[0] // 2
    block = pltpu.VMEM((4, row_count, facing, pts), jnp.float32)
    return pl.pallas_call(
        exchange_kernel,
        out_shape=jax.ShapeDtypeStruct(part.shape, jnp.float32),
        in_specs=[pl.BlockSpec(memory_space=pltpu.VMEM)] * 3,
        out_specs=pl.BlockSpec(memory_space=pltpu.VMEM),
        scratch_shapes=[
            block,
            block,
            pltpu.SemaphoreType.DMA((4,)),
            pltpu.SemaphoreType.DMA((4,)),
        ],
        compiler_params=pltpu.CompilerParams(
            collective_id=collective_id, has_side_effects=True
        ),
        name=f"exchange_{row_count}",
    )(part, hot, hot_t)


def split3(x):
    high = x.astype(jnp.bfloat16).astype(jnp.float32)
    mid = (x - high).astype(jnp.bfloat16).astype(jnp.float32)
    return [high, mid, x - high - mid]


def distance_features(vector):
    parts = [split3(x) for x in vector]
    high, mid, low = ([p[k] for p in parts] for k in range(3))
    norm = split3(vector[0] * vector[0] + vector[1] * vector[1] + vector[2] * vector[2])
    ones = [jnp.ones_like(vector[0])] * 3
    left = [-2.0 * x for x in high * 3] + norm + [-2.0 * x for x in mid * 2 + low] + ones
    right = high + mid + low + ones + high + mid + high + norm
    return left, right


def sum_features(value):
    parts = split3(value)
    ones = [jnp.ones_like(value)] * 3
    pad = [jnp.zeros_like(value)] * 2
    return parts + ones + pad, ones + parts + pad


def halves(x):
    high = x.astype(jnp.bfloat16)
    low = (x - high.astype(jnp.float32)).astype(jnp.bfloat16)
    return high, low


def two_columns(right_a, right_b):
    upper = jnp.concatenate([right_a, jnp.zeros_like(right_a)], axis=1)
    lower = jnp.concatenate([jnp.zeros_like(right_b), right_b], axis=1)
    return jnp.concatenate([upper, lower], axis=0)


def pass_kernel(force, first, pairs_ref, count_ref, weight_ref, place_ref, current_ref, *rest):
    rest = list(rest)
    coef_ref = rest.pop(0) if force else None
    out_ref = rest.pop(0)
    kept_ref = rest.pop(0) if first else None
    left_ref, right_ref, acc_ref = rest
    step = pl.program_id(0)
    total = count_ref[1]
    pts = weight_ref.shape[-1]
    extent = place_ref.shape[1]
    width = left_ref.shape[0] // extent
    used_rows = 64 if force else 48
    depth = 16 if force else 8
    rows, chunk = 32, 64

    @pl.when(step == 0)
    def _():
        acc_ref[...] = jnp.zeros(acc_ref.shape, jnp.float32)

        def fill(chunk, carry):
            at = pl.ds(pl.multiple_of(chunk * 8, 8), 8)
            groups = [distance_features([place_ref[k, at, :] for k in range(3)])]
            if force:
                groups.append(sum_features(coef_ref[0, at, :]))
            groups.append(distance_features([current_ref[k, at, :] for k in range(3)]))
            if force:
                groups.append(sum_features(coef_ref[1, at, :]))
            left = [x for group in groups for x in group[0]]
            right = [x for group in groups for x in group[1]]
            for k in range(used_rows):
                spot = pl.ds(chunk * (8 * width) + k, 8, stride=width)
                left_ref[spot, :] = left[k]
                right_ref[spot, :] = right[k]
            return carry

        lax.fori_loop(0, extent // 8, fill, 0)

    def one_slot(at):
        slot = step * GROUP + at
        source = pairs_ref[0, slot]
        target = pairs_ref[1, slot]
        used = slot < total
        left = left_ref[pl.ds(pl.multiple_of(source * width, 8), used_rows), :]
        right = right_ref[pl.ds(pl.multiple_of(target * width, 8), used_rows), :]
        if force:
            turned = jnp.transpose(left).astype(jnp.bfloat16)
            blank = jnp.zeros((32, 2 * pts), jnp.float32)
            still_right = jnp.concatenate(
                [two_columns(right[0:24], right[24:32]), blank], axis=0
            ).astype(jnp.bfloat16)
            moved_right = jnp.concatenate(
                [blank, two_columns(right[32:56], right[56:64])], axis=0
            ).astype(jnp.bfloat16)
        else:
            still = lax.dot_general(
                left.astype(jnp.bfloat16),
                two_columns(right[0:24], right[24:48]).astype(jnp.bfloat16),
                (((0,), (0,)), ((), ())),
                preferred_element_type=jnp.float32,
            )
        highs, lows = [], []
        column_sum = None
        for begin in range(0, pts, rows):
            cut = slice(begin, begin + rows)
            if force:
                local = slice(begin % chunk, begin % chunk + rows)
                if begin % chunk == 0:
                    points = turned[begin : begin + chunk]
                    still_cut = jnp.dot(points, still_right, preferred_element_type=jnp.float32)
                    moved_cut = jnp.dot(points, moved_right, preferred_element_type=jnp.float32)
                still_rows, moved_rows = still_cut[local], moved_cut[local]
            else:
                still_rows = still[cut]
            length_sq = jnp.maximum(still_rows[:, 0:pts], TINY)
            deformed_sq = jnp.maximum(
                moved_rows[:, 0:pts] if force else still_rows[:, pts:], TINY
            )
            length = length_sq * lax.rsqrt(length_sq)
            extension = deformed_sq * lax.rsqrt(deformed_sq) - length
            weight = weight_ref[at, cut, :]
            if first:
                p = lax.broadcasted_iota(jnp.int32, (rows, pts), 0) + begin
                q = lax.broadcasted_iota(jnp.int32, (rows, pts), 1)
                margin = jnp.where(source == target, 0, -2 * pts)
                weight = jnp.where(p + margin < q, weight.astype(jnp.float32), 0.0)
                weight = weight * jnp.exp2(-length_sq)
                kept_ref[at, cut, :] = weight
            if force:
                state = still_rows[:, pts:] * length + moved_rows[:, pts:] * extension
                term = weight * state * lax.rsqrt(deformed_sq + SOFTEN * LOG2E)
            else:
                term = weight * length * extension
                part = jnp.sum(term.reshape(rows // 8, 8, pts), axis=0)
                column_sum = part if column_sum is None else column_sum + part
            high, low = halves(term)
            highs.append(high)
            lows.append(low)
        high = jnp.concatenate(highs, axis=0)
        low = jnp.concatenate(lows, axis=0)
        wide = jnp.concatenate([high, low], axis=1)
        across = (((1,), (1,)), ((), ()))
        if force:
            tall = jnp.concatenate([high, low], axis=0)
            target_rows = right[32:48].astype(jnp.bfloat16)
            begin = pl.multiple_of(source * width, 8) + 32
            source_rows = right_ref[pl.ds(begin, 16), :].astype(jnp.bfloat16)
            to_source = lax.dot_general(
                jnp.concatenate([target_rows, target_rows], axis=1),
                wide,
                across,
                preferred_element_type=jnp.float32,
            )
            to_target = jnp.dot(
                jnp.concatenate([source_rows, source_rows], axis=1),
                tall,
                preferred_element_type=jnp.float32,
            )
        else:
            pick = (lax.broadcasted_iota(jnp.int32, (16, 2 * pts), 0) == 0).astype(jnp.bfloat16)
            to_source = lax.dot_general(pick, wide, across, preferred_element_type=jnp.float32)[0:8]
            to_target = column_sum
        return (
            jnp.where(used, source, extent) * depth,
            jnp.where(used, target, extent) * depth,
            to_source,
            to_target,
        )

    @pl.when(step * GROUP < total)
    def _():
        def turn(index, carry):
            found = [one_slot(index * UNROLL + k) for k in range(UNROLL)]
            for source, target, to_source, to_target in found:
                acc_ref[pl.ds(pl.multiple_of(source, 8), depth), :] += to_source
                acc_ref[pl.ds(pl.multiple_of(target, 8), depth), :] += to_target
            return carry

        lax.fori_loop(0, GROUP // UNROLL, turn, 0)

    @pl.when(step == pl.num_programs(0) - 1)
    def _():
        def finish(chunk, carry):
            at = pl.ds(pl.multiple_of(chunk * 8, 8), 8)

            def row(k):
                return acc_ref[pl.ds(chunk * (8 * depth) + k, 8, stride=depth), :]

            if force:
                count = row(9)
                for k in range(3):
                    moment = row(k) + row(3 + k) + row(6 + k)
                    out_ref[k, at, :] = (moment - current_ref[k, at, :] * count) * (1.0 / SCALE)
            else:
                out_ref[0, at, :] = sum(row(k) for k in range(1, 8)) + row(0)
            return carry

        lax.fori_loop(0, extent // 8, finish, 0)


def run_pass(force, first, pairs, counts, weight, *point_data):
    slots, pts = weight.shape[0], weight.shape[-1]
    extent = point_data[0].shape[1]
    out_rows = 3 if force else 1
    width, depth = (72, 16) if force else (56, 8)

    def slab(i, pairs_ref, count_ref):
        last = (count_ref[1] + GROUP - 1) // GROUP - 1
        return (jnp.minimum(i, last), 0, 0)

    def whole(*_):
        return (0, 0, 0)

    in_specs = [pl.BlockSpec((GROUP, pts, pts), slab)]
    in_specs += [pl.BlockSpec(x.shape, whole, pipeline_mode=pl.Buffered(1)) for x in point_data]
    out_shape = [jax.ShapeDtypeStruct((out_rows, extent, pts), jnp.float32)]
    out_specs = [pl.BlockSpec((out_rows, extent, pts), whole)]
    if first:
        out_shape.append(jax.ShapeDtypeStruct(weight.shape, jnp.float32))
        out_specs.append(pl.BlockSpec((GROUP, pts, pts), slab))
    return pl.pallas_call(
        functools.partial(pass_kernel, force, first),
        grid_spec=pltpu.PrefetchScalarGridSpec(
            num_scalar_prefetch=2,
            grid=(slots // GROUP,),
            in_specs=in_specs,
            out_specs=out_specs,
            scratch_shapes=[
                pltpu.VMEM((extent * width, pts), jnp.float32),
                pltpu.VMEM((extent * width, pts), jnp.float32),
                pltpu.VMEM(((extent + 1) * depth, pts), jnp.float32),
            ],
        ),
        out_shape=out_shape,
        compiler_params=pltpu.CompilerParams(
            dimension_semantics=("arbitrary",), vmem_limit_bytes=48 * 1024 * 1024
        ),
        name="force_pass" if force else "dilatation_pass",
    )(pairs, counts, weight, *point_data)


def body(
    position, displacement, velocity, bulk, shear, volume, edges, block_pairs, block_counts, damage
):
    points = damage.shape[-1]
    clusters = position.shape[-1] // points
    facing = edges.shape[-1]

    def rows_of(quantity):
        return quantity.reshape(-1, clusters, points)

    vol, bulk_c, shear_c = rows_of(volume), rows_of(bulk), rows_of(shear)
    table = jnp.concatenate(
        [
            rows_of(position),
            rows_of(displacement),
            rows_of(velocity),
            (3.0 * bulk_c - 5.0 * shear_c) / vol,
            15.0 * shear_c / vol,
            vol,
        ],
        axis=0,
    )
    pairs = block_pairs[0, 0]
    counts = block_counts[0, 0]
    weight = damage[0, 0]
    hot = (edges[0, 0].reshape(-1)[:, None] == jnp.arange(clusters, dtype=jnp.int32)).astype(
        jnp.bfloat16
    )

    hot_t = jnp.concatenate([hot.T] * 3, axis=1)
    hot = jnp.concatenate([hot] * 3, axis=1)
    padded = jnp.concatenate(
        [table, jnp.zeros((table.shape[0], 2 * facing, points), jnp.float32)], axis=1
    )
    full = exchange(padded, hot, hot_t, 0)
    place, moving, speed = full[0:3], full[3:6], full[6:9]
    dil_coef, dev_coef, vol = full[9:10], full[10:11], full[11:12]
    vol = jnp.where(vol == 0.0, 1.0, vol)
    still = place * SCALE
    for step in range(TIME_STEPS):
        current = (place + moving) * SCALE
        results = run_pass(False, step == 0, pairs, counts, weight, still, current)
        if step == 0:
            weight = results[1]
        theta = (3.0 / LOG2E) * exchange(results[0], hot, hot_t, 1) / vol
        coef = jnp.concatenate([dil_coef * theta, dev_coef], axis=0)
        (partials,) = run_pass(True, False, pairs, counts, weight, still, current, coef)
        force = exchange(partials, hot, hot_t, 2)
        speed = speed + TIMESTEP * force
        moving = moving + TIMESTEP * speed
    return (
        moving[:, :clusters].reshape(displacement.shape),
        speed[:, :clusters].reshape(velocity.shape),
        theta[:, :clusters].reshape(volume.shape),
    )


def solution(mesh):
    wide = P(None, "circ", "axial", None)
    flat = P("circ", "axial", None)
    pairs = P("circ", "axial", None, None)
    return jax.shard_map(
        body,
        mesh=mesh,
        in_specs=(wide, wide, wide, flat, flat, flat, pairs, pairs, flat, P("circ", "axial", None, None, None)),
        out_specs=(wide, wide, flat),
        check_vma=False,
    )
```
